32 devices in a mesh: dp: 4 (over y, x), tensor: 8 (over z, core).
Axes of the slice: x: 2, y: 2, z: 4, core: 2. Of those that a mesh axis runs over, the one named last changes fastest.
Arguments:
- drafted: bfloat16 [512, 8, 4096], P('dp', None, 'tensor'), may hold values from -6 to 6
- norm_gain: float32 [4096], replicated, may hold values from 0.25 to 1.75
- w_in: bfloat16 [4096, 3, 4096], P(None, None, 'tensor'), may hold values from -0.09375 to 0.09375
- conv_taps: float32 [3, 3, 4096], P(None, None, 'tensor'), may hold values from -2 to 2
- decay: float32 [4096], P('tensor'), may hold values from 0.2 to 0.98
- w_out: bfloat16 [4096, 4096], P('tensor'), may hold values from -0.09375 to 0.09375
- queue_tails: bfloat16 [512, 2, 3, 4096], P('dp', None, None, 'tensor'), may hold values from -6 to 6
- states: float32 [512, 4096], P('dp', 'tensor'), may hold values from -6 to 6
- accepted: int32 [512], P('dp'), may hold values from 0 to 8
- owner_map: int32 [512], P('dp'), may hold values from 0 to 511, as said below
Outputs:
- mixed: bfloat16 [512, 8, 4096], P(('dp', 'tensor'))
- new_tails: bfloat16 [512, 2, 3, 4096], P('dp', None, None, 'tensor')
- new_states: float32 [512, 4096], P('dp', 'tensor')
The draws below stay inside these ranges and needn't reach their ends.
Inputs may be any that keep to these rules, and one draw needn't show every extreme that they name: owner_map names every row once; the rows of each index of dp go 32 to each index of dp, that is to each block of 128 rows.
All inputs are finite; a program needn't handle non-finite values.
Results may differ from the reference program's by a relative error of at most 0.008.
Values may be sent and summed in bfloat16 or wider, within the bound.
No kernel may reach another device: no remote copies, remote signals or barrier semaphores. Data moves between devices by JAX's collectives and lax.ppermute only.
A program may use at most 128 MiB of HBM per device.

```python
import math
import jax
import jax.numpy as jnp
from jax import lax

D = 4096
K = 8
TAPS = 3
TAIL = 2
R_DEV = 128
ROWS = 512
SENDS = 32
N_DP = 4


def draw_owner_map(key, part):
    key = jax.random.fold_in(key, 7)
    first, second = jax.random.split(key)
    slot_order = jax.vmap(lambda k: jax.random.permutation(k, R_DEV))(jax.random.split(first, N_DP))
    grouped = slot_order.reshape(N_DP, N_DP, SENDS).transpose(1, 0, 2)
    targets = (jnp.arange(N_DP, dtype=jnp.int32)[None, :, None] * R_DEV + grouped).reshape(N_DP, R_DEV)
    row_order = jax.vmap(lambda k: jax.random.permutation(k, R_DEV))(jax.random.split(second, N_DP))
    result = jnp.zeros((N_DP, R_DEV), jnp.int32)
    result = result.at[jnp.arange(N_DP)[:, None], row_order].set(targets.astype(jnp.int32))
    return result.reshape(ROWS)


def set_ends(array, stream_key, smallest, top_value):
    longest = array.shape.index(max(array.shape))
    spots = []
    for shift in (0, 1):
        where = [jax.random.randint(jax.random.fold_in(stream_key, axis), (), 0, length) for axis, length in enumerate(array.shape)]
        where[longest] = (where[longest] + shift) % array.shape[longest]
        spots.append(tuple(where))
    return array.at[spots[0]].set(smallest).at[spots[1]].set(top_value)


def steps_of(own_key, shape, pieces, low, high):
    factor_of = 1.0
    for position, parts in pieces:
        draws = jax.random.uniform(jax.random.fold_in(jax.random.fold_in(own_key, 6), position), (parts,), jnp.float32, low / len(pieces), high / len(pieces))
        factor_of = factor_of * jnp.repeat(jnp.exp(draws), shape[position] // parts).reshape((-1,) + (1,) * (len(shape) - 1 - position))
    return factor_of


def normal_values(stream_key, extent, scale, bound, cuts=(), kind=jnp.bfloat16):
    loudness = steps_of(stream_key, extent, cuts, -0.22, 0.18) if cuts else 1.0
    values = jax.random.normal(stream_key, extent, jnp.float32) * scale * loudness
    return jnp.minimum(jnp.maximum(values, -bound), bound).astype(kind)


def setup_inputs(seed: int = 0) -> dict:
    arg_keys = jax.random.split(jax.random.key(seed), 11)
    drafted = normal_values(arg_keys[0], (ROWS, K, D), 1.0, 6.0, ((0, 4), (2, 8)))
    norm_gain = jnp.clip(1.0 + 0.15 * jax.random.normal(arg_keys[1], (D,), jnp.float32), 0.25, 1.75)
    w_in = normal_values(arg_keys[2], (D, 3, D), D ** -0.5, 0.09375, ((2, 8),))
    conv_taps = normal_values(arg_keys[3], (TAPS, 3, D), 0.5, 2.0, ((2, 8),), jnp.float32)
    decay = jnp.clip(jnp.exp(math.log(0.98) - 1.5892352 * jax.random.uniform(arg_keys[4], (D,), jnp.float32) ** steps_of(arg_keys[4], (D,), ((0, 8),), -0.2, 0.2)), 0.2, 0.98)
    w_out = normal_values(arg_keys[5], (D, D), D ** -0.5, 0.09375, ((0, 8),))
    queue_tails = normal_values(arg_keys[6], (ROWS, TAIL, 3, D), 1.0, 6.0, ((0, 4), (3, 8)))
    states = normal_values(arg_keys[7], (ROWS, D), 1.0, 6.0, ((0, 4), (1, 8)), jnp.float32)
    accepted = set_ends(jax.random.randint(arg_keys[8], (ROWS,), 0, K + 1), jax.random.fold_in(arg_keys[8], 1), 0, K).astype(jnp.int32)
    owner_map = draw_owner_map(jax.random.fold_in(arg_keys[10], 71), 0)
    return dict(drafted=drafted, norm_gain=norm_gain, w_in=w_in, conv_taps=conv_taps, decay=decay, w_out=w_out, queue_tails=queue_tails, states=states, accepted=accepted, owner_map=owner_map)


def verify_block(drafted, tails, states, accepted, norm_gain, w_in, conv_taps, decay, w_out):
    rows = drafted.shape[0]
    full = drafted.astype(jnp.float32)
    meansq = lax.optimization_barrier(jnp.mean(full * full, axis=-1, keepdims=True))
    normed = (full * lax.rsqrt(meansq + 1e-05) * norm_gain).astype(jnp.bfloat16)
    branches = jnp.dot(normed.reshape(rows * K, D), w_in.reshape(D, 3 * D), preferred_element_type=jnp.float32)
    branches = branches.astype(jnp.bfloat16).reshape(rows, K, 3, D)
    window = jnp.concatenate([tails, branches], axis=1)
    wide = window.astype(jnp.float32)
    filtered = jnp.zeros((rows, K, 3, D), jnp.float32)
    for tap in range(TAPS):
        filtered = filtered + conv_taps[tap] * wide[:, TAIL - tap:TAIL - tap + K]
    query = filtered[:, :, 0]
    keys = filtered[:, :, 1]
    values = filtered[:, :, 2]
    state = states
    history = [states]
    outputs = []
    for step in range(K):
        state = decay * state + keys[:, step] * values[:, step]
        history.append(state)
        outputs.append(query[:, step] * state)
    gated = jnp.stack(outputs, axis=1).astype(jnp.bfloat16)
    product = jnp.dot(gated.reshape(rows * K, D), w_out, preferred_element_type=jnp.float32)
    mixed = (full + product.reshape(rows, K, D)).astype(jnp.bfloat16)
    index = accepted[:, None] + jnp.arange(TAIL, dtype=jnp.int32)[None, :]
    new_tail = jnp.take_along_axis(window, index[:, :, None, None], axis=1)
    stacked = jnp.stack(history, axis=1)
    new_state = jnp.take_along_axis(stacked, accepted[:, None, None], axis=1)[:, 0]
    return (mixed, new_tail, new_state)

def reference(drafted, norm_gain, w_in, conv_taps, decay, w_out, queue_tails, states, accepted, owner_map):

    def one(block):
        return verify_block(block[0], block[1], block[2], block[3], norm_gain, w_in, conv_taps, decay, w_out)
    blocks = (drafted.reshape(N_DP, R_DEV, K, D), queue_tails.reshape(N_DP, R_DEV, TAIL, 3, D), states.reshape(N_DP, R_DEV, D), accepted.reshape(N_DP, R_DEV))
    mixed, tails_done, states_done = lax.map(one, blocks)
    mixed = mixed.reshape(ROWS, K, D)
    tails_done = tails_done.reshape(ROWS, TAIL, 3, D)
    states_done = states_done.reshape(ROWS, D)
    new_tails = jnp.zeros_like(tails_done).at[owner_map].set(tails_done)
    new_states = jnp.zeros_like(states_done).at[owner_map].set(states_done)
    return (mixed, new_tails, new_states)
```

```python
import functools
import jax
import jax.numpy as jnp
from jax import lax
from jax.experimental import pallas as pl
from jax.experimental.pallas import tpu as pltpu
from jax.sharding import PartitionSpec as P


AHEAD = 4
COST = 40


def chunk_kernel(
    nz, choices, tail_len, taps_n, steps, rows, local, width, block, share_rows,
    meta, *refs
):
    n_in = sum(choices)
    pieces = [refs[sum(choices[:k]):sum(choices[:k + 1])] for k in range(nz)]
    (w_own, w_sib, o_own, o_sib, gain, taps, decay, tails, states, accepted) = refs[n_in:n_in + 10]
    outs = refs[n_in + 10:]
    terms = outs[:nz]
    commit = outs[nz]
    xs, ns, wbuf, wob, br, gf, gs, pf, xsem, wsem, osem = outs[nz + 1:]
    is_end, core = meta[0], meta[1]
    tokens = rows * steps
    unit = share_rows * steps

    def piece_copy(slot, half, ref):
        place = meta[2 + slot] * 2 + (core if half == 0 else 1 - core)
        at = pl.multiple_of(place * local, 128)
        return pltpu.make_async_copy(ref.at[half], xs.at[:, pl.ds(at, local)], xsem.at[slot, half])

    for slot in range(nz):
        for half in range(2):
            if choices[slot] == 1:
                piece_copy(slot, half, pieces[slot][0]).start()
            else:
                @pl.when(is_end == 0)
                def _(slot=slot, half=half):
                    piece_copy(slot, half, pieces[slot][0]).start()

                @pl.when(is_end == 1)
                def _(slot=slot, half=half):
                    piece_copy(slot, half, pieces[slot][1]).start()

    half_k, half_o = width // 2, local // 2
    stream = []
    for index in range(6):
        for part in range(2):
            at = pl.ds(part * half_k, half_k)
            src = (w_own, w_sib)[index // 3].at[index % 3, at]
            stream.append(pltpu.make_async_copy(src, wbuf.at[index, at], wsem.at[2 * index + part]))
    for index in range(2):
        for part in range(2):
            src = (o_own, o_sib)[index].at[pl.ds(part * half_o, half_o)]
            dst = wob.at[pl.ds(index * local + part * half_o, half_o)]
            stream.append(pltpu.make_async_copy(src, dst, osem.at[2 * index + part]))
    for copy in stream[:AHEAD]:
        copy.start()

    def take(number):
        stream[number].wait()
        if number + AHEAD < len(stream):
            stream[number + AHEAD].start()

    for slot in range(nz):
        for half in range(2):
            piece_copy(slot, half, pieces[slot][0]).wait()

    def normalise(index, carry):
        at = pl.ds(pl.multiple_of(index * 16, 16), 16)
        wide = xs[at, :].astype(jnp.float32)
        meansq = jnp.mean(wide * wide, axis=-1, keepdims=True)
        ns[at, :] = (wide * lax.rsqrt(meansq + 1e-05) * gain[...]).astype(jnp.bfloat16)
        return carry

    lax.fori_loop(0, tokens // 16, normalise, 0, unroll=4)

    for block_index in range(2):
        for branch in range(3):
            take(6 * block_index + 2 * branch)
            take(6 * block_index + 2 * branch + 1)
            product = jnp.dot(ns[...], wbuf[block_index * 3 + branch], preferred_element_type=jnp.float32)
            product = product.astype(jnp.bfloat16).astype(jnp.float32)
            for lane in range(block // 128):
                br[branch, lane] = product[:, lane * 128:(lane + 1) * 128]
        for lane in range(0, block, 128):
            lanes = pl.ds(lane, 128)
            taken = jnp.broadcast_to(accepted[...], (rows, 128))
            window = []
            for s in range(tail_len):
                window.append([tails[block_index, s * 3 + j, :, lanes].astype(jnp.float32) for j in range(3)])
            state = states[block_index, :, lanes]
            kept = state
            rate = decay[block_index, :, lanes]
            weight = [[taps[block_index, pl.ds(tap * 3 + j, 1), lanes] for j in range(3)] for tap in range(taps_n)]
            tail = [[window[i][j] for j in range(3)] for i in range(tail_len)]
            for i in range(tail_len):
                for s in range(i + 1, tail_len):
                    for j in range(3):
                        tail[i][j] = jnp.where(taken == s - i, window[s][j], tail[i][j])
            for step in range(steps):
                window.append([br[j, lane // 128, pl.ds(step, rows, stride=steps), :] for j in range(3)])
                s = tail_len + step
                for i in range(tail_len):
                    if s - i <= steps:
                        mask = taken == s - i
                        for j in range(3):
                            tail[i][j] = jnp.where(mask, window[s][j], tail[i][j])
                mixed = []
                for j in range(3):
                    total = weight[0][j] * window[s][j]
                    for tap in range(1, taps_n):
                        total = total + weight[tap][j] * window[s - tap][j]
                    mixed.append(total)
                state = rate * state + mixed[1] * mixed[2]
                kept = jnp.where(taken == step + 1, state, kept)
                gf[lane // 128, pl.ds(step, rows, stride=steps), :] = mixed[0] * state
            for i in range(tail_len):
                for j in range(3):
                    plane = (j * tail_len + i) * block + lane
                    commit[block_index, :, plane:plane + 128] = tail[i][j].astype(jnp.bfloat16)
            high = kept.astype(jnp.bfloat16)
            plane = 3 * tail_len * block + lane
            commit[block_index, :, plane:plane + 128] = high
            low = (kept - high.astype(jnp.float32)).astype(jnp.bfloat16)
            commit[block_index, :, plane + block:plane + block + 128] = low
        for lane in range(block // 128):
            gs[block_index, :, pl.ds(lane * 128, 128)] = gf[lane].astype(jnp.bfloat16)

    for number in range(12, 16):
        take(number)
    gated = jnp.concatenate([gs[b] for b in range(2)], axis=1)
    wide_out = 512
    for at in range(0, width, wide_out):
        columns = pl.ds(at, wide_out)
        pf[...] = jnp.dot(gated, wob[:, columns], preferred_element_type=jnp.float32)
        for slot in range(nz):
            picked = pl.ds(pl.multiple_of(meta[2 + slot] * unit, 16), unit)
            value = pf[picked, :]
            if slot == 0:
                terms[slot][:, columns] = value + xs[picked, columns].astype(jnp.float32)
            else:
                terms[slot][:, columns] = value.astype(jnp.bfloat16)


def run_chunk(nz, meta, slots, w_own, w_sib, o_own, o_sib, gain, taps, decay, tails, states, accepted, steps, share_rows, taps_n, tail_len):
    choices = tuple(len(slot) for slot in slots)
    pieces = [piece for slot in slots for piece in slot]
    _, tokens, local = pieces[0].shape
    width = w_own.shape[1]
    block = local
    blocks = 2 * local // block
    rows = tokens // steps
    unit = share_rows * steps
    anywhere = pl.BlockSpec(memory_space=pl.ANY)
    vmem = pl.BlockSpec(memory_space=pltpu.VMEM)
    out_shape = [jax.ShapeDtypeStruct((unit, width), jnp.float32)]
    out_shape += [jax.ShapeDtypeStruct((unit, width), jnp.bfloat16)] * (nz - 1)
    out_shape += [
        jax.ShapeDtypeStruct((blocks, rows, (tail_len * 3 + 2) * block), jnp.bfloat16),
    ]
    return pl.pallas_call(
        functools.partial(
            chunk_kernel, nz, choices, tail_len, taps_n, steps, rows, local, width, block, share_rows
        ),
        out_shape=out_shape,
        in_specs=[pl.BlockSpec(memory_space=pltpu.SMEM)] + [anywhere] * (len(pieces) + 4) + [vmem] * 6,
        out_specs=[vmem] * len(out_shape),
        scratch_shapes=[
            pltpu.VMEM((tokens, width), jnp.bfloat16),
            pltpu.VMEM((tokens, width), jnp.bfloat16),
            pltpu.VMEM((6, width, block), jnp.bfloat16),
            pltpu.VMEM((2 * local, width), jnp.bfloat16),
            pltpu.VMEM((3, block // 128, tokens, 128), jnp.float32),
            pltpu.VMEM((block // 128, tokens, 128), jnp.float32),
            pltpu.VMEM((blocks, tokens, block), jnp.bfloat16),
            pltpu.VMEM((tokens, 512), jnp.float32),
            pltpu.SemaphoreType.DMA((nz, 2)),
            pltpu.SemaphoreType.DMA((12,)),
            pltpu.SemaphoreType.DMA((4,)),
        ],
        compiler_params=pltpu.CompilerParams(vmem_limit_bytes=58 * 1024 * 1024),
        cost_estimate=pl.CostEstimate(
            flops=COST * tokens * width * local, bytes_accessed=4 * tokens * width, transcendentals=0
        ),
    )(meta, *pieces, w_own, w_sib, o_own, o_sib, gain, taps, decay, tails, states, accepted)


def per_device(
    n_tensor, n_dp,
    drafted, norm_gain, w_in, conv_taps, decay, w_out, queue_tails, states, accepted, owner_map
):
    rows, steps, local = drafted.shape
    taps_n = conv_taps.shape[0]
    tail_len = queue_tails.shape[1]
    width = w_in.shape[0]
    nz = n_tensor // 2
    share = rows // n_tensor
    block = local
    me = lax.axis_index("tensor")
    z, core = me // 2, me % 2
    is_end = jnp.logical_or(z == 0, z == nz - 1)

    swap_pairs = [(t, t ^ 1) for t in range(n_tensor)]

    def permute(value, links, what):
        with jax.named_scope(what):
            return lax.ppermute(value, "tensor", links)

    def swap(value, what):
        return permute(value, swap_pairs, what)

    def chips(links):
        return [(2 * a + c, 2 * b + c) for a, b in links for c in (0, 1)]

    sizes = [share // 2, share - share // 2]
    parts = len(sizes)
    cuts = [slice(sum(sizes[:p]), sum(sizes[:p + 1])) for p in range(parts)]

    def mine(array):
        return lax.dynamic_index_in_dim(array, core, 1, keepdims=False)

    def other(array):
        return lax.dynamic_index_in_dim(array, 1 - core, 1, keepdims=False)

    by_core = drafted.reshape(nz, 2, share, steps, local)
    here, there = mine(by_core), other(by_core)
    arrived = swap(there, "swap_tokens")
    held = []
    for part in range(parts):
        cut, size = cuts[part], sizes[part]
        held.append(jnp.stack([
            here[:, cut].reshape(nz * size * steps, local),
            arrived[:, cut].reshape(nz * size * steps, local),
        ]))

    held, conv_taps, decay, queue_tails, states, owner_map = lax.optimization_barrier(
        (held, conv_taps, decay, queue_tails, states, owner_map)
    )
    small = jnp.concatenate([conv_taps.reshape(taps_n * 3, local), decay[None]], axis=0)
    small_sib = swap(small, "swap_taps")
    tails_core = jnp.transpose(queue_tails, (1, 2, 0, 3)).reshape(tail_len * 3, nz, 2, share, local)
    tails_here = lax.dynamic_index_in_dim(tails_core, core, 2, keepdims=False)
    tails_sib = swap(lax.dynamic_index_in_dim(tails_core, 1 - core, 2, keepdims=False), "swap_tails")
    states_core = states.reshape(nz, 2, share, local)
    states_sib = swap(other(states_core), "swap_states")
    states_here = mine(states_core)

    w_in, w_out, small_sib, tails_sib, states_sib = lax.optimization_barrier(
        (w_in, w_out, small_sib, tails_sib, states_sib)
    )
    w_own = jnp.transpose(w_in, (1, 0, 2))
    w_sib = swap(w_own, "swap_w_in")
    o_sib = swap(w_out, "swap_w_out")

    def blocked(own, sib):
        both = jnp.concatenate([own, sib], axis=-1)
        cut = both.reshape(*both.shape[:-1], 2 * local // block, block)
        return jnp.moveaxis(cut, -2, 0)

    small_all = blocked(small, small_sib)
    taps_all, decay_all = small_all[:, :-1], small_all[:, -1:]
    accepted_here = mine(accepted.reshape(nz, 2, share))

    line = nz == 4
    if line:
        order = [z, z ^ 1, jnp.where(z < 2, 2, 1), jnp.where(z < 2, 3, 0)]
        ends = chips([(0, 1), (1, 0), (2, 3), (3, 2)])
        outward = chips([(1, 0), (2, 3)])
        inward = chips([(0, 1), (3, 2)])
        between = chips([(1, 2), (2, 1)])
        middle = between + [(0, 1), (1, 0), (6, 7), (7, 6)]
        across = chips([(0, 3), (3, 0)]) + [(2, 3), (3, 2), (4, 5), (5, 4)]
        skip_in = chips([(0, 2), (3, 1)])
        skip_out = chips([(2, 0), (1, 3)])
    else:
        order = [(z - k) % nz for k in range(nz)]
        ring = chips([(k, (k + 1) % nz) for k in range(nz)])
    meta = jnp.stack([is_end.astype(jnp.int32), core] + order).astype(jnp.int32)

    def ordered(array):
        return jnp.concatenate(
            [array[:, cut].reshape(-1) for cut in cuts]
        )

    if line:
        x0, x1 = held
        e1, m1 = permute(x0, ends, "gather0_e1"), permute(x0, between, "gather0_m1")
        e1, m1, owner_map = lax.optimization_barrier((e1, m1, owner_map))
    owner_core = owner_map.reshape(nz, 2, share)
    owner = jnp.concatenate([ordered(mine(owner_core)), ordered(other(owner_core))])
    sends = rows // n_dp
    target, slot = owner // rows, owner % rows
    same = target[:, None] == target[None, :]
    index = jnp.arange(rows, dtype=jnp.int32)
    rank = jnp.sum(jnp.where(same & (index[None, :] < index[:, None]), 1, 0), axis=1)
    place = target * sends + rank
    pick = place[None, :] == index[:, None]
    slot_out = jnp.sum(jnp.where(pick, slot[None, :], 0), axis=1)
    slot_in = lax.all_to_all(slot_out.reshape(n_dp, sends), "dp", split_axis=0, concat_axis=0, tiled=True)
    put = (slot_in.reshape(rows)[None, :] == index[:, None]).astype(jnp.bfloat16)
    pick = pick.astype(jnp.bfloat16)

    gain = norm_gain[None]
    sides = []
    for cut, size in zip(cuts, sizes):
        sides.append((
            blocked(
                tails_here[:, :, cut].reshape(tail_len * 3, nz * size, local),
                tails_sib[:, :, cut].reshape(tail_len * 3, nz * size, local),
            ),
            blocked(
                states_here[:, cut].reshape(nz * size, local), states_sib[:, cut].reshape(nz * size, local)
            ),
            accepted_here[:, cut].reshape(nz * size, 1),
        ))

    barrier = lax.optimization_barrier

    def add(a, b):
        return (a.astype(jnp.float32) + b.astype(jnp.float32)).astype(jnp.bfloat16)

    def run(part, slots):
        tails_part, states_part, accepted_part = sides[part]
        return run_chunk(
            nz, meta, slots, w_own, w_sib, w_out, o_sib, gain, taps_all, decay_all,
            tails_part, states_part, accepted_part, steps, sizes[part], taps_n, tail_len,
        )

    if line:
        e2 = permute(m1, outward, "gather0_e2")
        m2 = permute(e1, between, "gather0_m2")
        m2, e2, x1, sides, taps_all, decay_all, meta, pick, put = barrier(
            (m2, e2, x1, sides, taps_all, decay_all, meta, pick, put)
        )
        e3 = permute(m2, outward, "gather0_e3")
        g1 = permute(x1, middle, "gather1_m1")
        e3, g1, x1 = barrier((e3, g1, x1))
        f1 = permute(x1, ends, "gather1_e1")
        g2, f3 = permute(x1, skip_in, "gather1_skip"), permute(x1, across, "gather1_across")
        f2 = permute(g1, outward, "gather1_e2")
        first = run(0, [(x0,), (e1,), (m1, e2), (m2, e3)])
        own0, near0, mid0, far0, commit0 = first
        near0, mid0, far0, f1, f2, f3, g2 = barrier((near0, mid0, far0, f1, f2, f3, g2))
        mid0_in = permute(mid0, inward, "sum0_mid_in")
        near0_in = permute(near0, ends, "sum0_near")
        far0_in, skip0_in = permute(far0, across, "sum0_across"), permute(far0, skip_out, "sum0_skip")
        own1, near1, mid1, far1, commit1 = run(1, [(x1,), (f1,), (g1, f2), (g2, f3)])
        far1_in, mid1_in = permute(far1, inward, "sum1_far_in"), permute(mid1, inward, "sum1_mid_in")
        near1, commit1, mid0_in, near0_in, far0_in, skip0_in = barrier(
            (near1, commit1, mid0_in, near0_in, far0_in, skip0_in)
        )
        mid0_on = permute(add(mid0, mid0_in), middle, "sum0_mid_on")
        second = [own1, near1, mid1, far1, commit1]
        results = [first, second]
    else:
        results = []
        for part in range(parts):
            slots = [(held[part],)]
            for _ in range(nz - 1):
                slots.append((permute(slots[-1][0], ring, f"gather{part}"),))
            results.append(run(part, slots))

    packed = jnp.concatenate([r[-1] for r in results], axis=1)
    packed = jnp.concatenate([packed[0], swap(packed[1], "swap_commit")], axis=0)
    sent = jnp.dot(pick, packed, preferred_element_type=jnp.float32).astype(jnp.bfloat16)
    if line:
        far1_on = permute(add(far1, far1_in), middle, "sum1_far_on")
        mid1, sent = barrier((add(mid1, mid1_in), sent))
    got = lax.all_to_all(sent, "dp", split_axis=0, concat_axis=0, tiled=True)
    if line:
        mid1_on = permute(mid1, middle, "sum1_mid_on")
        near1 = add(near1, jnp.where(is_end, 0, far1_on))
        near1_in = permute(near1, ends, "sum1_near")
        wide = lambda value: value.astype(jnp.float32)
        total0 = own0 + wide(near0_in) + jnp.where(is_end, wide(far0_in) + wide(skip0_in), wide(mid0_on))
        total1 = own1 + wide(near1_in) + jnp.where(is_end, 0, wide(mid1_on))
        totals = [total0, total1]
    else:
        totals = []
        for terms in results:
            flow = terms[1]
            for k in range(2, nz):
                flow = add(terms[k], permute(flow, ring, "sum"))
            totals.append(terms[0] + permute(flow, ring, "sum").astype(jnp.float32))
    mixed = [
        total.astype(jnp.bfloat16).reshape(size, steps, width) for total, size in zip(totals, sizes)
    ]
    mixed = jnp.concatenate(mixed, axis=0)

    placed = jnp.dot(put, got, preferred_element_type=jnp.float32)
    edge = 3 * tail_len * local
    new_tails = placed[:, :edge].astype(jnp.bfloat16).reshape(rows, 3, tail_len, local)
    new_tails = jnp.transpose(new_tails, (0, 2, 1, 3))
    new_states = placed[:, edge:edge + local] + placed[:, edge + local:]
    return (mixed, new_tails, new_states)


def solution(mesh):
    return jax.shard_map(
        functools.partial(per_device, mesh.shape["tensor"], mesh.shape["dp"]),
        mesh=mesh,
        in_specs=(
            P("dp", None, "tensor"),
            P(),
            P(None, None, "tensor"),
            P(None, None, "tensor"),
            P("tensor"),
            P("tensor", None),
            P("dp", None, None, "tensor"),
            P("dp", "tensor"),
            P("dp"),
            P("dp"),
        ),
        out_specs=(
            P(("dp", "tensor"), None, None),
            P("dp", None, None, "tensor"),
            P("dp", "tensor"),
        ),
        check_vma=False,
    )
```

```python
import functools
import jax
import jax.numpy as jnp
from jax import lax
from jax.experimental import pallas as pl
from jax.experimental.pallas import tpu as pltpu
from jax.sharding import PartitionSpec as P


AHEAD = 4
COST = 40


def chunk_kernel(
    nz, choices, tail_len, taps_n, steps, rows, local, width, block, share_rows,
    meta, *refs
):
    n_in = sum(choices)
    pieces = [refs[sum(choices[:k]):sum(choices[:k + 1])] for k in range(nz)]
    (w_own, w_sib, o_own, o_sib, gain, taps, decay, tails, states, accepted) = refs[n_in:n_in + 10]
    outs = refs[n_in + 10:]
    terms = outs[:nz]
    commit = outs[nz]
    xs, ns, wbuf, wob, br, gf, gs, pf, xsem, wsem, osem = outs[nz + 1:]
    is_end, core = meta[0], meta[1]
    tokens = rows * steps
    unit = share_rows * steps

    def piece_copy(slot, half, ref):
        place = meta[2 + slot] * 2 + (core if half == 0 else 1 - core)
        at = pl.multiple_of(place * local, 128)
        return pltpu.make_async_copy(ref.at[half], xs.at[:, pl.ds(at, local)], xsem.at[slot, half])

    for slot in range(nz):
        for half in range(2):
            if choices[slot] == 1:
                piece_copy(slot, half, pieces[slot][0]).start()
            else:
                @pl.when(is_end == 0)
                def _(slot=slot, half=half):
                    piece_copy(slot, half, pieces[slot][0]).start()

                @pl.when(is_end == 1)
                def _(slot=slot, half=half):
                    piece_copy(slot, half, pieces[slot][1]).start()

    half_k, half_o = width // 2, local // 2
    stream = []
    for index in range(6):
        for part in range(2):
            at = pl.ds(part * half_k, half_k)
            src = (w_own, w_sib)[index // 3].at[index % 3, at]
            stream.append(pltpu.make_async_copy(src, wbuf.at[index, at], wsem.at[2 * index + part]))
    for index in range(2):
        for part in range(2):
            src = (o_own, o_sib)[index].at[pl.ds(part * half_o, half_o)]
            dst = wob.at[pl.ds(index * local + part * half_o, half_o)]
            stream.append(pltpu.make_async_copy(src, dst, osem.at[2 * index + part]))
    for copy in stream[:AHEAD]:
        copy.start()

    def take(number):
        stream[number].wait()
        if number + AHEAD < len(stream):
            stream[number + AHEAD].start()

    for slot in range(nz):
        for half in range(2):
            piece_copy(slot, half, pieces[slot][0]).wait()

    def normalise(index, carry):
        at = pl.ds(pl.multiple_of(index * 16, 16), 16)
        wide = xs[at, :].astype(jnp.float32)
        meansq = jnp.mean(wide * wide, axis=-1, keepdims=True)
        ns[at, :] = (wide * lax.rsqrt(meansq + 1e-05) * gain[...]).astype(jnp.bfloat16)
        return carry

    lax.fori_loop(0, tokens // 16, normalise, 0, unroll=4)

    for block_index in range(2):
        for branch in range(3):
            take(6 * block_index + 2 * branch)
            take(6 * block_index + 2 * branch + 1)
            product = jnp.dot(ns[...], wbuf[block_index * 3 + branch], preferred_element_type=jnp.float32)
            product = product.astype(jnp.bfloat16).astype(jnp.float32)
            for lane in range(block // 128):
                br[branch, lane] = product[:, lane * 128:(lane + 1) * 128]
        for lane in range(0, block, 128):
            lanes = pl.ds(lane, 128)
            taken = jnp.broadcast_to(accepted[...], (rows, 128))
            window = []
            for s in range(tail_len):
                window.append([tails[block_index, s * 3 + j, :, lanes].astype(jnp.float32) for j in range(3)])
            state = states[block_index, :, lanes]
            kept = state
            rate = decay[block_index, :, lanes]
            weight = [[taps[block_index, pl.ds(tap * 3 + j, 1), lanes] for j in range(3)] for tap in range(taps_n)]
            tail = [[window[i][j] for j in range(3)] for i in range(tail_len)]
            for i in range(tail_len):
                for s in range(i + 1, tail_len):
                    for j in range(3):
                        tail[i][j] = jnp.where(taken == s - i, window[s][j], tail[i][j])
            for step in range(steps):
                window.append([br[j, lane // 128, pl.ds(step, rows, stride=steps), :] for j in range(3)])
                s = tail_len + step
                for i in range(tail_len):
                    if s - i <= steps:
                        mask = taken == s - i
                        for j in range(3):
                            tail[i][j] = jnp.where(mask, window[s][j], tail[i][j])
                mixed = []
                for j in range(3):
                    total = weight[0][j] * window[s][j]
                    for tap in range(1, taps_n):
                        total = total + weight[tap][j] * window[s - tap][j]
                    mixed.append(total)
                state = rate * state + mixed[1] * mixed[2]
                kept = jnp.where(taken == step + 1, state, kept)
                gf[lane // 128, pl.ds(step, rows, stride=steps), :] = mixed[0] * state
            for i in range(tail_len):
                for j in range(3):
                    plane = (j * tail_len + i) * block + lane
                    commit[block_index, :, plane:plane + 128] = tail[i][j].astype(jnp.bfloat16)
            high = kept.astype(jnp.bfloat16)
            plane = 3 * tail_len * block + lane
            commit[block_index, :, plane:plane + 128] = high
            low = (kept - high.astype(jnp.float32)).astype(jnp.bfloat16)
            commit[block_index, :, plane + block:plane + block + 128] = low
        for lane in range(block // 128):
            gs[block_index, :, pl.ds(lane * 128, 128)] = gf[lane].astype(jnp.bfloat16)

    for number in range(12, 16):
        take(number)
    gated = jnp.concatenate([gs[b] for b in range(2)], axis=1)
    wide_out = 512
    for at in range(0, width, wide_out):
        columns = pl.ds(at, wide_out)
        pf[...] = jnp.dot(gated, wob[:, columns], preferred_element_type=jnp.float32)
        for slot in range(nz):
            picked = pl.ds(pl.multiple_of(meta[2 + slot] * unit, 16), unit)
            value = pf[picked, :]
            if slot == 0:
                terms[slot][:, columns] = value + xs[picked, columns].astype(jnp.float32)
            else:
                terms[slot][:, columns] = value.astype(jnp.bfloat16)


def run_chunk(nz, meta, slots, w_own, w_sib, o_own, o_sib, gain, taps, decay, tails, states, accepted, steps, share_rows, taps_n, tail_len):
    choices = tuple(len(slot) for slot in slots)
    pieces = [piece for slot in slots for piece in slot]
    _, tokens, local = pieces[0].shape
    width = w_own.shape[1]
    block = local
    blocks = 2 * local // block
    rows = tokens // steps
    unit = share_rows * steps
    anywhere = pl.BlockSpec(memory_space=pl.ANY)
    vmem = pl.BlockSpec(memory_space=pltpu.VMEM)
    out_shape = [jax.ShapeDtypeStruct((unit, width), jnp.float32)]
    out_shape += [jax.ShapeDtypeStruct((unit, width), jnp.bfloat16)] * (nz - 1)
    out_shape += [
        jax.ShapeDtypeStruct((blocks, rows, (tail_len * 3 + 2) * block), jnp.bfloat16),
    ]
    return pl.pallas_call(
        functools.partial(
            chunk_kernel, nz, choices, tail_len, taps_n, steps, rows, local, width, block, share_rows
        ),
        out_shape=out_shape,
        in_specs=[pl.BlockSpec(memory_space=pltpu.SMEM)] + [anywhere] * (len(pieces) + 4) + [vmem] * 6,
        out_specs=[vmem] * len(out_shape),
        scratch_shapes=[
            pltpu.VMEM((tokens, width), jnp.bfloat16),
            pltpu.VMEM((tokens, width), jnp.bfloat16),
            pltpu.VMEM((6, width, block), jnp.bfloat16),
            pltpu.VMEM((2 * local, width), jnp.bfloat16),
            pltpu.VMEM((3, block // 128, tokens, 128), jnp.float32),
            pltpu.VMEM((block // 128, tokens, 128), jnp.float32),
            pltpu.VMEM((blocks, tokens, block), jnp.bfloat16),
            pltpu.VMEM((tokens, 512), jnp.float32),
            pltpu.SemaphoreType.DMA((nz, 2)),
            pltpu.SemaphoreType.DMA((12,)),
            pltpu.SemaphoreType.DMA((4,)),
        ],
        compiler_params=pltpu.CompilerParams(vmem_limit_bytes=58 * 1024 * 1024),
        cost_estimate=pl.CostEstimate(
            flops=COST * tokens * width * local, bytes_accessed=4 * tokens * width, transcendentals=0
        ),
    )(meta, *pieces, w_own, w_sib, o_own, o_sib, gain, taps, decay, tails, states, accepted)


def per_device(
    n_tensor, n_dp,
    drafted, norm_gain, w_in, conv_taps, decay, w_out, queue_tails, states, accepted, owner_map
):
    rows, steps, local = drafted.shape
    taps_n = conv_taps.shape[0]
    tail_len = queue_tails.shape[1]
    width = w_in.shape[0]
    nz = n_tensor // 2
    share = rows // n_tensor
    block = local
    me = lax.axis_index("tensor")
    z, core = me // 2, me % 2
    is_end = jnp.logical_or(z == 0, z == nz - 1)

    swap_pairs = [(t, t ^ 1) for t in range(n_tensor)]

    def permute(value, links, what):
        with jax.named_scope(what):
            return lax.ppermute(value, "tensor", links)

    def swap(value, what):
        return permute(value, swap_pairs, what)

    def chips(links):
        return [(2 * a + c, 2 * b + c) for a, b in links for c in (0, 1)]

    sizes = [share // 2, share - share // 2]
    parts = len(sizes)
    cuts = [slice(sum(sizes[:p]), sum(sizes[:p + 1])) for p in range(parts)]

    def mine(array):
        return lax.dynamic_index_in_dim(array, core, 1, keepdims=False)

    def other(array):
        return lax.dynamic_index_in_dim(array, 1 - core, 1, keepdims=False)

    by_core = drafted.reshape(nz, 2, share, steps, local)
    here, there = mine(by_core), other(by_core)
    arrived = swap(there, "swap_tokens")
    held = []
    for part in range(parts):
        cut, size = cuts[part], sizes[part]
        held.append(jnp.stack([
            here[:, cut].reshape(nz * size * steps, local),
            arrived[:, cut].reshape(nz * size * steps, local),
        ]))

    held, conv_taps, decay, queue_tails, states, owner_map = lax.optimization_barrier(
        (held, conv_taps, decay, queue_tails, states, owner_map)
    )
    small = jnp.concatenate([conv_taps.reshape(taps_n * 3, local), decay[None]], axis=0)
    small_sib = swap(small, "swap_taps")
    tails_core = jnp.transpose(queue_tails, (1, 2, 0, 3)).reshape(tail_len * 3, nz, 2, share, local)
    tails_here = lax.dynamic_index_in_dim(tails_core, core, 2, keepdims=False)
    tails_sib = swap(lax.dynamic_index_in_dim(tails_core, 1 - core, 2, keepdims=False), "swap_tails")
    states_core = states.reshape(nz, 2, share, local)
    states_sib = swap(other(states_core), "swap_states")
    states_here = mine(states_core)

    def blocked(own, sib):
        both = jnp.concatenate([own, sib], axis=-1)
        cut = both.reshape(*both.shape[:-1], 2 * local // block, block)
        return jnp.moveaxis(cut, -2, 0)

    accepted_here = mine(accepted.reshape(nz, 2, share))

    line = nz == 4
    if line:
        order = [z, z ^ 1, jnp.where(z < 2, 2, 1), jnp.where(z < 2, 3, 0)]
        ends = chips([(0, 1), (1, 0), (2, 3), (3, 2)])
        outward = chips([(1, 0), (2, 3)])
        inward = chips([(0, 1), (3, 2)])
        between = chips([(1, 2), (2, 1)])
        middle = between + [(0, 1), (1, 0), (6, 7), (7, 6)]
        across = chips([(0, 3), (3, 0)]) + [(2, 3), (3, 2), (4, 5), (5, 4)]
        skip_in = chips([(0, 2), (3, 1)])
        skip_out = chips([(2, 0), (1, 3)])
    else:
        order = [(z - k) % nz for k in range(nz)]
        ring = chips([(k, (k + 1) % nz) for k in range(nz)])
    meta = jnp.stack([is_end.astype(jnp.int32), core] + order).astype(jnp.int32)

    def ordered(array):
        return jnp.concatenate(
            [array[:, cut].reshape(-1) for cut in cuts]
        )

    def commit_order(owner_map):
        owner_core = owner_map.reshape(nz, 2, share)
        owner = jnp.concatenate([ordered(mine(owner_core)), ordered(other(owner_core))])
        sends = rows // n_dp
        target, slot = owner // rows, owner % rows
        same = target[:, None] == target[None, :]
        index = jnp.arange(rows, dtype=jnp.int32)
        rank = jnp.sum(jnp.where(same & (index[None, :] < index[:, None]), 1, 0), axis=1)
        place = target * sends + rank
        pick = place[None, :] == index[:, None]
        slot_out = jnp.sum(jnp.where(pick, slot[None, :], 0), axis=1)
        slot_in = lax.all_to_all(slot_out.reshape(n_dp, sends), "dp", split_axis=0, concat_axis=0, tiled=True)
        put = (slot_in.reshape(rows)[None, :] == index[:, None]).astype(jnp.bfloat16)
        pick = pick.astype(jnp.bfloat16)
        return pick, put

    if line:
        x0, x1 = held
        e1, m1 = permute(x0, ends, "gather0_e1"), permute(x0, middle, "gather0_m1")
        e1, m1, owner_map, w_in, w_out, small_sib, tails_sib, states_sib = lax.optimization_barrier(
            (e1, m1, owner_map, w_in, w_out, small_sib, tails_sib, states_sib)
        )
    w_own = jnp.transpose(w_in, (1, 0, 2))
    w_sib = swap(w_own, "swap_w_in")
    o_sib = swap(w_out, "swap_w_out")
    small_all = blocked(small, small_sib)
    taps_all, decay_all = small_all[:, :-1], small_all[:, -1:]
    gain = norm_gain[None]
    sides = []
    for cut, size in zip(cuts, sizes):
        sides.append((
            blocked(
                tails_here[:, :, cut].reshape(tail_len * 3, nz * size, local),
                tails_sib[:, :, cut].reshape(tail_len * 3, nz * size, local),
            ),
            blocked(
                states_here[:, cut].reshape(nz * size, local), states_sib[:, cut].reshape(nz * size, local)
            ),
            accepted_here[:, cut].reshape(nz * size, 1),
        ))

    barrier = lax.optimization_barrier

    def add(a, b):
        return (a.astype(jnp.float32) + b.astype(jnp.float32)).astype(jnp.bfloat16)

    def run(part, slots):
        tails_part, states_part, accepted_part = sides[part]
        return run_chunk(
            nz, meta, slots, w_own, w_sib, w_out, o_sib, gain, taps_all, decay_all,
            tails_part, states_part, accepted_part, steps, sizes[part], taps_n, tail_len,
        )

    if line:
        e2 = permute(m1, outward, "gather0_e2")
        m2 = permute(e1, between, "gather0_m2")
        m2, e2, x1, sides, taps_all, decay_all, meta, owner_map = barrier(
            (m2, e2, x1, sides, taps_all, decay_all, meta, owner_map)
        )
        pick, put = commit_order(owner_map)
        e3 = permute(m2, outward, "gather0_e3")
        g1 = permute(x1, middle, "gather1_m1")
        e3, g1, x1, pick, put = barrier((e3, g1, x1, pick, put))
        f1 = permute(x1, ends, "gather1_e1")
        g2, f3 = permute(x1, skip_in, "gather1_skip"), permute(x1, across, "gather1_across")
        f2 = permute(g1, outward, "gather1_e2")
        first = run(0, [(x0,), (e1,), (m1, e2), (m2, e3)])
        own0, near0, mid0, far0, commit0 = first
        mid0, far0, f1, f2, f3, g2 = barrier((mid0, far0, f1, f2, f3, g2))
        mid0_in = permute(mid0, inward, "sum0_mid_in")
        far0_in, skip0_in = permute(far0, across, "sum0_across"), permute(far0, skip_out, "sum0_skip")
        own1, near1, mid1, far1, commit1 = run(1, [(x1,), (f1,), (g1, f2), (g2, f3)])
        far1_in = permute(far1, inward, "sum1_far_in")
        near1, commit1, mid0_in, far0_in, skip0_in = barrier((near1, commit1, mid0_in, far0_in, skip0_in))
        mid0_on = permute(add(mid0, mid0_in), middle, "sum0_mid_on")
        near0, mid1, far1_in, mid0_on = barrier((near0, mid1, far1_in, mid0_on))
        mid1_in = permute(mid1, inward, "sum1_mid_in")
        near0_in = permute(near0, ends, "sum0_near")
        second = [own1, near1, mid1, far1, commit1]
        results = [first, second]
    else:
        pick, put = commit_order(owner_map)
        results = []
        for part in range(parts):
            slots = [(held[part],)]
            for _ in range(nz - 1):
                slots.append((permute(slots[-1][0], ring, f"gather{part}"),))
            results.append(run(part, slots))

    packed = jnp.concatenate([r[-1] for r in results], axis=1)
    packed = jnp.concatenate([packed[0], swap(packed[1], "swap_commit")], axis=0)
    sent = jnp.dot(pick, packed, preferred_element_type=jnp.float32).astype(jnp.bfloat16)
    if line:
        far1_on = permute(add(far1, far1_in), middle, "sum1_far_on")
        mid1, sent = barrier((add(mid1, mid1_in), sent))
    got = lax.all_to_all(sent, "dp", split_axis=0, concat_axis=0, tiled=True)
    if line:
        mid1_on = permute(mid1, middle, "sum1_mid_on")
        near1 = add(near1, jnp.where(is_end, 0, far1_on))
        near1_in = permute(near1, ends, "sum1_near")
        wide = lambda value: value.astype(jnp.float32)
        total0 = own0 + wide(near0_in) + jnp.where(is_end, wide(far0_in) + wide(skip0_in), wide(mid0_on))
        total1 = own1 + wide(near1_in) + jnp.where(is_end, 0, wide(mid1_on))
        totals = [total0, total1]
    else:
        totals = []
        for terms in results:
            flow = terms[1]
            for k in range(2, nz):
                flow = add(terms[k], permute(flow, ring, "sum"))
            totals.append(terms[0] + permute(flow, ring, "sum").astype(jnp.float32))
    mixed = [
        total.astype(jnp.bfloat16).reshape(size, steps, width) for total, size in zip(totals, sizes)
    ]
    mixed = jnp.concatenate(mixed, axis=0)

    placed = jnp.dot(put, got, preferred_element_type=jnp.float32)
    edge = 3 * tail_len * local
    new_tails = placed[:, :edge].astype(jnp.bfloat16).reshape(rows, 3, tail_len, local)
    new_tails = jnp.transpose(new_tails, (0, 2, 1, 3))
    new_states = placed[:, edge:edge + local] + placed[:, edge + local:]
    return (mixed, new_tails, new_states)


def solution(mesh):
    return jax.shard_map(
        functools.partial(per_device, mesh.shape["tensor"], mesh.shape["dp"]),
        mesh=mesh,
        in_specs=(
            P("dp", None, "tensor"),
            P(),
            P(None, None, "tensor"),
            P(None, None, "tensor"),
            P("tensor"),
            P("tensor", None),
            P("dp", None, None, "tensor"),
            P("dp", "tensor"),
            P("dp"),
            P("dp"),
        ),
        out_specs=(
            P(("dp", "tensor"), None, None),
            P("dp", None, None, "tensor"),
            P("dp", "tensor"),
        ),
        check_vma=False,
    )
```

```python
import functools
import jax
import jax.numpy as jnp
from jax import lax
from jax.experimental import pallas as pl
from jax.experimental.pallas import tpu as pltpu
from jax.sharding import PartitionSpec as P


AHEAD = 4
COST = 40


def chunk_kernel(
    nz, choices, tail_len, taps_n, steps, rows, local, width, block, share_rows,
    meta, *refs
):
    n_in = sum(choices)
    pieces = [refs[sum(choices[:k]):sum(choices[:k + 1])] for k in range(nz)]
    (w_own, w_sib, o_own, o_sib, gain, taps, decay, tails, states, accepted) = refs[n_in:n_in + 10]
    outs = refs[n_in + 10:]
    terms_out, commit_out = outs[:nz], outs[nz]
    xs, ns, wbuf, wob, br, gf, gs, pf, own, rest, commit, xsem, wsem, osem, tsem, csem = outs[nz + 1:]
    is_end, core = meta[0], meta[1]
    tokens = rows * steps
    unit = share_rows * steps

    def piece_copy(slot, half, ref):
        place = meta[2 + slot] * 2 + (core if half == 0 else 1 - core)
        at = pl.multiple_of(place * local, 128)
        return pltpu.make_async_copy(ref.at[half], xs.at[:, pl.ds(at, local)], xsem.at[slot, half])

    for slot in range(nz):
        for half in range(2):
            if choices[slot] == 1:
                piece_copy(slot, half, pieces[slot][0]).start()
            else:
                @pl.when(is_end == 0)
                def _(slot=slot, half=half):
                    piece_copy(slot, half, pieces[slot][0]).start()

                @pl.when(is_end == 1)
                def _(slot=slot, half=half):
                    piece_copy(slot, half, pieces[slot][1]).start()

    half_k, half_o = width // 2, local // 2
    stream = []
    for index in range(6):
        for part in range(2):
            at = pl.ds(part * half_k, half_k)
            src = (w_own, w_sib)[index // 3].at[index % 3, at]
            stream.append(pltpu.make_async_copy(src, wbuf.at[index, at], wsem.at[2 * index + part]))
    for index in range(2):
        for part in range(2):
            src = (o_own, o_sib)[index].at[pl.ds(part * half_o, half_o)]
            dst = wob.at[pl.ds(index * local + part * half_o, half_o)]
            stream.append(pltpu.make_async_copy(src, dst, osem.at[2 * index + part]))
    for copy in stream[:AHEAD]:
        copy.start()

    def take(number):
        stream[number].wait()
        if number + AHEAD < len(stream):
            stream[number + AHEAD].start()

    for slot in range(nz):
        for half in range(2):
            piece_copy(slot, half, pieces[slot][0]).wait()

    def normalise(index, carry):
        at = pl.ds(pl.multiple_of(index * 16, 16), 16)
        wide = xs[at, :].astype(jnp.float32)
        meansq = jnp.mean(wide * wide, axis=-1, keepdims=True)
        ns[at, :] = (wide * lax.rsqrt(meansq + 1e-05) * gain[...]).astype(jnp.bfloat16)
        return carry

    lax.fori_loop(0, tokens // 16, normalise, 0, unroll=4)

    for block_index in range(2):
        for branch in range(3):
            take(6 * block_index + 2 * branch)
            take(6 * block_index + 2 * branch + 1)
            product = jnp.dot(ns[...], wbuf[block_index * 3 + branch], preferred_element_type=jnp.float32)
            product = product.astype(jnp.bfloat16).astype(jnp.float32)
            for lane in range(block // 128):
                br[branch, lane] = product[:, lane * 128:(lane + 1) * 128]
        for lane in range(0, block, 128):
            lanes = pl.ds(lane, 128)
            taken = jnp.broadcast_to(accepted[...], (rows, 128))
            window = []
            for s in range(tail_len):
                window.append([tails[block_index, s * 3 + j, :, lanes].astype(jnp.float32) for j in range(3)])
            state = states[block_index, :, lanes]
            kept = state
            rate = decay[block_index, :, lanes]
            weight = [[taps[block_index, pl.ds(tap * 3 + j, 1), lanes] for j in range(3)] for tap in range(taps_n)]
            tail = [[window[i][j] for j in range(3)] for i in range(tail_len)]
            for i in range(tail_len):
                for s in range(i + 1, tail_len):
                    for j in range(3):
                        tail[i][j] = jnp.where(taken == s - i, window[s][j], tail[i][j])
            for step in range(steps):
                window.append([br[j, lane // 128, pl.ds(step, rows, stride=steps), :] for j in range(3)])
                s = tail_len + step
                for i in range(tail_len):
                    if s - i <= steps:
                        mask = taken == s - i
                        for j in range(3):
                            tail[i][j] = jnp.where(mask, window[s][j], tail[i][j])
                mixed = []
                for j in range(3):
                    total = weight[0][j] * window[s][j]
                    for tap in range(1, taps_n):
                        total = total + weight[tap][j] * window[s - tap][j]
                    mixed.append(total)
                state = rate * state + mixed[1] * mixed[2]
                kept = jnp.where(taken == step + 1, state, kept)
                gf[lane // 128, pl.ds(step, rows, stride=steps), :] = mixed[0] * state
            for i in range(tail_len):
                for j in range(3):
                    plane = (j * tail_len + i) * block + lane
                    commit[block_index, :, plane:plane + 128] = tail[i][j].astype(jnp.bfloat16)
            high = kept.astype(jnp.bfloat16)
            plane = 3 * tail_len * block + lane
            commit[block_index, :, plane:plane + 128] = high
            low = (kept - high.astype(jnp.float32)).astype(jnp.bfloat16)
            commit[block_index, :, plane + block:plane + block + 128] = low
        for lane in range(block // 128):
            gs[block_index, :, pl.ds(lane * 128, 128)] = gf[lane].astype(jnp.bfloat16)

    commit_copy = pltpu.make_async_copy(commit, commit_out, csem)
    commit_copy.start()
    for number in range(12, 16):
        take(number)
    gated = jnp.concatenate([gs[b] for b in range(2)], axis=1)
    wide_out, sent = 512, []
    for at in range(0, width, wide_out):
        columns = pl.ds(at, wide_out)
        pf[...] = jnp.dot(gated, wob[:, columns], preferred_element_type=jnp.float32)
        for slot in range(nz):
            picked = pl.ds(pl.multiple_of(meta[2 + slot] * unit, 16), unit)
            value = pf[picked, :]
            if slot == 0:
                own[:, columns] = value + xs[picked, columns].astype(jnp.float32)
            else:
                rest[slot - 1, :, columns] = value.astype(jnp.bfloat16)
        if (at + wide_out) % (width // 2) == 0:
            part = at // (width // 2)
            half = pl.ds(part * (width // 2), width // 2)
            for slot in range(nz):
                src = own if slot == 0 else rest.at[slot - 1]
                copy = pltpu.make_async_copy(src.at[:, half], terms_out[slot].at[:, half], tsem.at[part, slot])
                copy.start()
                sent.append(copy)
    for copy in sent:
        copy.wait()
    commit_copy.wait()


def run_chunk(nz, meta, slots, w_own, w_sib, o_own, o_sib, gain, taps, decay, tails, states, accepted, steps, share_rows, taps_n, tail_len):
    choices = tuple(len(slot) for slot in slots)
    pieces = [piece for slot in slots for piece in slot]
    _, tokens, local = pieces[0].shape
    width = w_own.shape[1]
    block = local
    blocks = 2 * local // block
    rows = tokens // steps
    unit = share_rows * steps
    anywhere = pl.BlockSpec(memory_space=pl.ANY)
    vmem = pl.BlockSpec(memory_space=pltpu.VMEM)
    out_shape = [jax.ShapeDtypeStruct((unit, width), jnp.float32)]
    out_shape += [jax.ShapeDtypeStruct((unit, width), jnp.bfloat16)] * (nz - 1)
    out_shape += [
        jax.ShapeDtypeStruct((blocks, rows, (tail_len * 3 + 2) * block), jnp.bfloat16),
    ]
    return pl.pallas_call(
        functools.partial(
            chunk_kernel, nz, choices, tail_len, taps_n, steps, rows, local, width, block, share_rows
        ),
        out_shape=out_shape,
        in_specs=[pl.BlockSpec(memory_space=pltpu.SMEM)] + [anywhere] * (len(pieces) + 4) + [vmem] * 6,
        out_specs=[anywhere] * len(out_shape),
        scratch_shapes=[
            pltpu.VMEM((tokens, width), jnp.bfloat16),
            pltpu.VMEM((tokens, width), jnp.bfloat16),
            pltpu.VMEM((6, width, block), jnp.bfloat16),
            pltpu.VMEM((2 * local, width), jnp.bfloat16),
            pltpu.VMEM((3, block // 128, tokens, 128), jnp.float32),
            pltpu.VMEM((block // 128, tokens, 128), jnp.float32),
            pltpu.VMEM((blocks, tokens, block), jnp.bfloat16),
            pltpu.VMEM((tokens, 512), jnp.float32),
            pltpu.VMEM((unit, width), jnp.float32),
            pltpu.VMEM((nz - 1, unit, width), jnp.bfloat16),
            pltpu.VMEM(out_shape[-1].shape, jnp.bfloat16),
            pltpu.SemaphoreType.DMA((nz, 2)),
            pltpu.SemaphoreType.DMA((12,)),
            pltpu.SemaphoreType.DMA((4,)),
            pltpu.SemaphoreType.DMA((2, nz)),
            pltpu.SemaphoreType.DMA,
        ],
        compiler_params=pltpu.CompilerParams(vmem_limit_bytes=58 * 1024 * 1024),
        cost_estimate=pl.CostEstimate(
            flops=COST * tokens * width * local, bytes_accessed=4 * tokens * width, transcendentals=0
        ),
    )(meta, *pieces, w_own, w_sib, o_own, o_sib, gain, taps, decay, tails, states, accepted)


def per_device(
    n_tensor, n_dp,
    drafted, norm_gain, w_in, conv_taps, decay, w_out, queue_tails, states, accepted, owner_map
):
    rows, steps, local = drafted.shape
    taps_n = conv_taps.shape[0]
    tail_len = queue_tails.shape[1]
    width = w_in.shape[0]
    nz = n_tensor // 2
    share = rows // n_tensor
    block = local
    me = lax.axis_index("tensor")
    z, core = me // 2, me % 2
    is_end = jnp.logical_or(z == 0, z == nz - 1)

    swap_pairs = [(t, t ^ 1) for t in range(n_tensor)]

    def permute(value, links, what):
        with jax.named_scope(what):
            return lax.ppermute(value, "tensor", links)

    def swap(value, what):
        return permute(value, swap_pairs, what)

    def chips(links):
        return [(2 * a + c, 2 * b + c) for a, b in links for c in (0, 1)]

    sizes = [share // 2, share - share // 2]
    parts = len(sizes)
    cuts = [slice(sum(sizes[:p]), sum(sizes[:p + 1])) for p in range(parts)]

    def mine(array):
        return lax.dynamic_index_in_dim(array, core, 1, keepdims=False)

    def other(array):
        return lax.dynamic_index_in_dim(array, 1 - core, 1, keepdims=False)

    by_core = drafted.reshape(nz, 2, share, steps, local)
    here, there = mine(by_core), other(by_core)
    arrived = swap(there, "swap_tokens")
    held = []
    for part in range(parts):
        cut, size = cuts[part], sizes[part]
        held.append(jnp.stack([
            here[:, cut].reshape(nz * size * steps, local),
            arrived[:, cut].reshape(nz * size * steps, local),
        ]))

    held, conv_taps, decay, queue_tails, states, owner_map = lax.optimization_barrier(
        (held, conv_taps, decay, queue_tails, states, owner_map)
    )
    small = jnp.concatenate([conv_taps.reshape(taps_n * 3, local), decay[None]], axis=0)
    small_sib = swap(small, "swap_taps")
    tails_core = jnp.transpose(queue_tails, (1, 2, 0, 3)).reshape(tail_len * 3, nz, 2, share, local)
    tails_here = lax.dynamic_index_in_dim(tails_core, core, 2, keepdims=False)
    tails_sib = swap(lax.dynamic_index_in_dim(tails_core, 1 - core, 2, keepdims=False), "swap_tails")
    states_core = states.reshape(nz, 2, share, local)
    states_sib = swap(other(states_core), "swap_states")
    states_here = mine(states_core)

    def blocked(own, sib):
        both = jnp.concatenate([own, sib], axis=-1)
        cut = both.reshape(*both.shape[:-1], 2 * local // block, block)
        return jnp.moveaxis(cut, -2, 0)

    accepted_here = mine(accepted.reshape(nz, 2, share))

    line = nz == 4
    if line:
        order = [z, z ^ 1, jnp.where(z < 2, 2, 1), jnp.where(z < 2, 3, 0)]
        ends = chips([(0, 1), (1, 0), (2, 3), (3, 2)])
        outward = chips([(1, 0), (2, 3)])
        inward = chips([(0, 1), (3, 2)])
        between = chips([(1, 2), (2, 1)])
        middle = between + [(0, 1), (1, 0), (6, 7), (7, 6)]
        across = chips([(0, 3), (3, 0)]) + [(2, 3), (3, 2), (4, 5), (5, 4)]
        skip_in = chips([(0, 2), (3, 1)])
        skip_out = chips([(2, 0), (1, 3)])
    else:
        order = [(z - k) % nz for k in range(nz)]
        ring = chips([(k, (k + 1) % nz) for k in range(nz)])
    meta = jnp.stack([is_end.astype(jnp.int32), core] + order).astype(jnp.int32)

    def ordered(array):
        return jnp.concatenate(
            [array[:, cut].reshape(-1) for cut in cuts]
        )

    def commit_order(owner_map):
        owner_core = owner_map.reshape(nz, 2, share)
        owner = jnp.concatenate([ordered(mine(owner_core)), ordered(other(owner_core))])
        sends = rows // n_dp
        target, slot = owner // rows, owner % rows
        same = target[:, None] == target[None, :]
        index = jnp.arange(rows, dtype=jnp.int32)
        rank = jnp.sum(jnp.where(same & (index[None, :] < index[:, None]), 1, 0), axis=1)
        place = target * sends + rank
        pick = place[None, :] == index[:, None]
        slot_out = jnp.sum(jnp.where(pick, slot[None, :], 0), axis=1)
        slot_in = lax.all_to_all(slot_out.reshape(n_dp, sends), "dp", split_axis=0, concat_axis=0, tiled=True)
        put = (slot_in.reshape(rows)[None, :] == index[:, None]).astype(jnp.bfloat16)
        pick = pick.astype(jnp.bfloat16)
        return pick, put

    if line:
        x0, x1 = held
        e1, m1 = permute(x0, ends, "gather0_e1"), permute(x0, middle, "gather0_m1")
        e1, m1, owner_map, w_in, w_out, small_sib, tails_sib, states_sib = lax.optimization_barrier(
            (e1, m1, owner_map, w_in, w_out, small_sib, tails_sib, states_sib)
        )
    w_own = jnp.transpose(w_in, (1, 0, 2))
    w_sib = swap(w_own, "swap_w_in")
    o_sib = swap(w_out, "swap_w_out")
    small_all = blocked(small, small_sib)
    taps_all, decay_all = small_all[:, :-1], small_all[:, -1:]
    gain = norm_gain[None]
    sides = []
    for cut, size in zip(cuts, sizes):
        sides.append((
            blocked(
                tails_here[:, :, cut].reshape(tail_len * 3, nz * size, local),
                tails_sib[:, :, cut].reshape(tail_len * 3, nz * size, local),
            ),
            blocked(
                states_here[:, cut].reshape(nz * size, local), states_sib[:, cut].reshape(nz * size, local)
            ),
            accepted_here[:, cut].reshape(nz * size, 1),
        ))

    barrier = lax.optimization_barrier

    def add(a, b):
        return (a.astype(jnp.float32) + b.astype(jnp.float32)).astype(jnp.bfloat16)

    def run(part, slots):
        tails_part, states_part, accepted_part = sides[part]
        return run_chunk(
            nz, meta, slots, w_own, w_sib, w_out, o_sib, gain, taps_all, decay_all,
            tails_part, states_part, accepted_part, steps, sizes[part], taps_n, tail_len,
        )

    if line:
        e2 = permute(m1, outward, "gather0_e2")
        m2 = permute(e1, between, "gather0_m2")
        m2, x1, sides, taps_all, decay_all, meta, owner_map = barrier(
            (m2, x1, sides, taps_all, decay_all, meta, owner_map)
        )
        pick, put = commit_order(owner_map)
        e3 = permute(m2, outward, "gather0_e3")
        g1 = permute(x1, middle, "gather1_m1")
        e2, e3, g1, x1, pick, put = barrier((e2, e3, g1, x1, pick, put))
        f1 = permute(x1, ends, "gather1_e1")
        g2, f3 = permute(x1, skip_in, "gather1_skip"), permute(x1, across, "gather1_across")
        f2 = permute(g1, outward, "gather1_e2")
        first = run(0, [(x0,), (e1,), (m1, e2), (m2, e3)])
        own0, near0, mid0, far0, commit0 = first
        mid0, far0, f1, f2, f3, g2 = barrier((mid0, far0, f1, f2, f3, g2))
        mid0_in = permute(mid0, inward, "sum0_mid_in")
        far0_in, skip0_in = permute(far0, across, "sum0_across"), permute(far0, skip_out, "sum0_skip")
        own1, near1, mid1, far1, commit1 = run(1, [(x1,), (f1,), (g1, f2), (g2, f3)])
        far1_in = permute(far1, inward, "sum1_far_in")
        near1, commit1, mid0_in, far0_in, skip0_in = barrier((near1, commit1, mid0_in, far0_in, skip0_in))
        mid0_on = permute(add(mid0, mid0_in), middle, "sum0_mid_on")
        near0, mid1, far1_in, mid0_on = barrier((near0, mid1, far1_in, mid0_on))
        mid1_in = permute(mid1, inward, "sum1_mid_in")
        near0_in = permute(near0, ends, "sum0_near")
        second = [own1, near1, mid1, far1, commit1]
        results = [first, second]
    else:
        pick, put = commit_order(owner_map)
        results = []
        for part in range(parts):
            slots = [(held[part],)]
            for _ in range(nz - 1):
                slots.append((permute(slots[-1][0], ring, f"gather{part}"),))
            results.append(run(part, slots))

    packed = jnp.concatenate([r[-1] for r in results], axis=1)
    packed = jnp.concatenate([packed[0], swap(packed[1], "swap_commit")], axis=0)
    sent = jnp.dot(pick, packed, preferred_element_type=jnp.float32).astype(jnp.bfloat16)
    if line:
        far1_on = permute(add(far1, far1_in), middle, "sum1_far_on")
        mid1, sent = barrier((add(mid1, mid1_in), sent))
    got = lax.all_to_all(sent, "dp", split_axis=0, concat_axis=0, tiled=True)
    if line:
        mid1_on = permute(mid1, middle, "sum1_mid_on")
        near1 = add(near1, jnp.where(is_end, 0, far1_on))
        near1_in = permute(near1, ends, "sum1_near")
        wide = lambda value: value.astype(jnp.float32)
        total0 = own0 + wide(near0_in) + jnp.where(is_end, wide(far0_in) + wide(skip0_in), wide(mid0_on))
        total1 = own1 + wide(near1_in) + jnp.where(is_end, 0, wide(mid1_on))
        totals = [total0, total1]
    else:
        totals = []
        for terms in results:
            flow = terms[1]
            for k in range(2, nz):
                flow = add(terms[k], permute(flow, ring, "sum"))
            totals.append(terms[0] + permute(flow, ring, "sum").astype(jnp.float32))
    mixed = [
        total.astype(jnp.bfloat16).reshape(size, steps, width) for total, size in zip(totals, sizes)
    ]
    mixed = jnp.concatenate(mixed, axis=0)

    placed = jnp.dot(put, got, preferred_element_type=jnp.float32)
    edge = 3 * tail_len * local
    new_tails = placed[:, :edge].astype(jnp.bfloat16).reshape(rows, 3, tail_len, local)
    new_tails = jnp.transpose(new_tails, (0, 2, 1, 3))
    new_states = placed[:, edge:edge + local] + placed[:, edge + local:]
    return (mixed, new_tails, new_states)


def solution(mesh):
    return jax.shard_map(
        functools.partial(per_device, mesh.shape["tensor"], mesh.shape["dp"]),
        mesh=mesh,
        in_specs=(
            P("dp", None, "tensor"),
            P(),
            P(None, None, "tensor"),
            P(None, None, "tensor"),
            P("tensor"),
            P("tensor", None),
            P("dp", None, None, "tensor"),
            P("dp", "tensor"),
            P("dp"),
            P("dp"),
        ),
        out_specs=(
            P(("dp", "tensor"), None, None),
            P("dp", None, None, "tensor"),
            P("dp", "tensor"),
        ),
        check_vma=False,
    )
```

```python
import functools
import jax
import jax.numpy as jnp
from jax import lax
from jax.experimental import pallas as pl
from jax.experimental.pallas import tpu as pltpu
from jax.sharding import PartitionSpec as P


AHEAD = 4
COST = 40


def chunk_kernel(
    nz, choices, tail_len, taps_n, steps, rows, local, width, block, share_rows,
    meta, *refs
):
    n_in = sum(choices)
    pieces = [refs[sum(choices[:k]):sum(choices[:k + 1])] for k in range(nz)]
    (w_own, w_sib, o_own, o_sib, gain, taps, decay, tails, states, accepted) = refs[n_in:n_in + 10]
    outs = refs[n_in + 10:]
    terms_out, commit_out = outs[:nz], outs[nz]
    xs, ns, wbuf, wob, br, gf, gs, pf, own, rest, commit, xsem, wsem, osem, tsem, csem = outs[nz + 1:]
    is_end, core = meta[0], meta[1]
    tokens = rows * steps
    unit = share_rows * steps

    def piece_copy(slot, half, ref):
        place = meta[2 + slot] * 2 + (core if half == 0 else 1 - core)
        at = pl.multiple_of(place * local, 128)
        return pltpu.make_async_copy(ref.at[half], xs.at[:, pl.ds(at, local)], xsem.at[slot, half])

    for slot in range(nz):
        for half in range(2):
            if choices[slot] == 1:
                piece_copy(slot, half, pieces[slot][0]).start()
            else:
                @pl.when(is_end == 0)
                def _(slot=slot, half=half):
                    piece_copy(slot, half, pieces[slot][0]).start()

                @pl.when(is_end == 1)
                def _(slot=slot, half=half):
                    piece_copy(slot, half, pieces[slot][1]).start()

    half_k, half_o = width // 2, local // 2
    stream = []
    for index in range(6):
        for part in range(2):
            at = pl.ds(part * half_k, half_k)
            src = (w_own, w_sib)[index // 3].at[index % 3, at]
            stream.append(pltpu.make_async_copy(src, wbuf.at[index, at], wsem.at[2 * index + part]))
    for index in range(2):
        for part in range(2):
            src = (o_own, o_sib)[index].at[pl.ds(part * half_o, half_o)]
            dst = wob.at[pl.ds(index * local + part * half_o, half_o)]
            stream.append(pltpu.make_async_copy(src, dst, osem.at[2 * index + part]))
    for copy in stream[:AHEAD]:
        copy.start()

    def take(number):
        stream[number].wait()
        if number + AHEAD < len(stream):
            stream[number + AHEAD].start()

    for slot in range(nz):
        for half in range(2):
            piece_copy(slot, half, pieces[slot][0]).wait()

    def normalise(index, carry):
        at = pl.ds(pl.multiple_of(index * 16, 16), 16)
        wide = xs[at, :].astype(jnp.float32)
        meansq = jnp.mean(wide * wide, axis=-1, keepdims=True)
        ns[at, :] = (wide * lax.rsqrt(meansq + 1e-05) * gain[...]).astype(jnp.bfloat16)
        return carry

    lax.fori_loop(0, tokens // 16, normalise, 0, unroll=4)

    for block_index in range(2):
        for branch in range(3):
            take(6 * block_index + 2 * branch)
            take(6 * block_index + 2 * branch + 1)
            product = jnp.dot(ns[...], wbuf[block_index * 3 + branch], preferred_element_type=jnp.float32)
            product = product.astype(jnp.bfloat16).astype(jnp.float32)
            for lane in range(block // 128):
                br[branch, lane] = product[:, lane * 128:(lane + 1) * 128]
        for lane in range(0, block, 128):
            lanes = pl.ds(lane, 128)
            taken = jnp.broadcast_to(accepted[...], (rows, 128))
            window = []
            for s in range(tail_len):
                window.append([tails[block_index, s * 3 + j, :, lanes].astype(jnp.float32) for j in range(3)])
            state = states[block_index, :, lanes]
            kept = state
            rate = decay[block_index, :, lanes]
            weight = [[taps[block_index, pl.ds(tap * 3 + j, 1), lanes] for j in range(3)] for tap in range(taps_n)]
            tail = [[window[i][j] for j in range(3)] for i in range(tail_len)]
            for i in range(tail_len):
                for s in range(i + 1, tail_len):
                    for j in range(3):
                        tail[i][j] = jnp.where(taken == s - i, window[s][j], tail[i][j])
            for step in range(steps):
                window.append([br[j, lane // 128, pl.ds(step, rows, stride=steps), :] for j in range(3)])
                s = tail_len + step
                for i in range(tail_len):
                    if s - i <= steps:
                        mask = taken == s - i
                        for j in range(3):
                            tail[i][j] = jnp.where(mask, window[s][j], tail[i][j])
                mixed = []
                for j in range(3):
                    total = weight[0][j] * window[s][j]
                    for tap in range(1, taps_n):
                        total = total + weight[tap][j] * window[s - tap][j]
                    mixed.append(total)
                state = rate * state + mixed[1] * mixed[2]
                kept = jnp.where(taken == step + 1, state, kept)
                gf[lane // 128, pl.ds(step, rows, stride=steps), :] = mixed[0] * state
            for i in range(tail_len):
                for j in range(3):
                    plane = (j * tail_len + i) * block + lane
                    commit[block_index, :, plane:plane + 128] = tail[i][j].astype(jnp.bfloat16)
            high = kept.astype(jnp.bfloat16)
            plane = 3 * tail_len * block + lane
            commit[block_index, :, plane:plane + 128] = high
            low = (kept - high.astype(jnp.float32)).astype(jnp.bfloat16)
            commit[block_index, :, plane + block:plane + block + 128] = low
        for lane in range(block // 128):
            gs[block_index, :, pl.ds(lane * 128, 128)] = gf[lane].astype(jnp.bfloat16)

    commit_copy = pltpu.make_async_copy(commit, commit_out, csem)
    commit_copy.start()
    for number in range(12, 16):
        take(number)
    gated = jnp.concatenate([gs[b] for b in range(2)], axis=1)
    wide_out, sent = 512, []
    for at in range(0, width, wide_out):
        columns = pl.ds(at, wide_out)
        pf[...] = jnp.dot(gated, wob[:, columns], preferred_element_type=jnp.float32)
        for slot in range(nz):
            picked = pl.ds(pl.multiple_of(meta[2 + slot] * unit, 16), unit)
            value = pf[picked, :]
            if slot == 0:
                own[:, columns] = value + xs[picked, columns].astype(jnp.float32)
            else:
                rest[slot - 1, :, columns] = value.astype(jnp.bfloat16)
        if (at + wide_out) % (width // 2) == 0:
            part = at // (width // 2)
            half = pl.ds(part * (width // 2), width // 2)
            for slot in range(nz):
                src = own if slot == 0 else rest.at[slot - 1]
                copy = pltpu.make_async_copy(src.at[:, half], terms_out[slot].at[:, half], tsem.at[part, slot])
                copy.start()
                sent.append(copy)
    for copy in sent:
        copy.wait()
    commit_copy.wait()


def run_chunk(nz, meta, slots, w_own, w_sib, o_own, o_sib, gain, taps, decay, tails, states, accepted, steps, share_rows, taps_n, tail_len):
    choices = tuple(len(slot) for slot in slots)
    pieces = [piece for slot in slots for piece in slot]
    _, tokens, local = pieces[0].shape
    width = w_own.shape[1]
    block = local
    blocks = 2 * local // block
    rows = tokens // steps
    unit = share_rows * steps
    anywhere = pl.BlockSpec(memory_space=pl.ANY)
    vmem = pl.BlockSpec(memory_space=pltpu.VMEM)
    out_shape = [jax.ShapeDtypeStruct((unit, width), jnp.float32)]
    out_shape += [jax.ShapeDtypeStruct((unit, width), jnp.bfloat16)] * (nz - 1)
    out_shape += [
        jax.ShapeDtypeStruct((blocks, rows, (tail_len * 3 + 2) * block), jnp.bfloat16),
    ]
    return pl.pallas_call(
        functools.partial(
            chunk_kernel, nz, choices, tail_len, taps_n, steps, rows, local, width, block, share_rows
        ),
        out_shape=out_shape,
        in_specs=[pl.BlockSpec(memory_space=pltpu.SMEM)] + [anywhere] * (len(pieces) + 4) + [vmem] * 6,
        out_specs=[anywhere] * len(out_shape),
        scratch_shapes=[
            pltpu.VMEM((tokens, width), jnp.bfloat16),
            pltpu.VMEM((tokens, width), jnp.bfloat16),
            pltpu.VMEM((6, width, block), jnp.bfloat16),
            pltpu.VMEM((2 * local, width), jnp.bfloat16),
            pltpu.VMEM((3, block // 128, tokens, 128), jnp.float32),
            pltpu.VMEM((block // 128, tokens, 128), jnp.float32),
            pltpu.VMEM((blocks, tokens, block), jnp.bfloat16),
            pltpu.VMEM((tokens, 512), jnp.float32),
            pltpu.VMEM((unit, width), jnp.float32),
            pltpu.VMEM((nz - 1, unit, width), jnp.bfloat16),
            pltpu.VMEM(out_shape[-1].shape, jnp.bfloat16),
            pltpu.SemaphoreType.DMA((nz, 2)),
            pltpu.SemaphoreType.DMA((12,)),
            pltpu.SemaphoreType.DMA((4,)),
            pltpu.SemaphoreType.DMA((2, nz)),
            pltpu.SemaphoreType.DMA,
        ],
        compiler_params=pltpu.CompilerParams(vmem_limit_bytes=58 * 1024 * 1024),
        cost_estimate=pl.CostEstimate(
            flops=COST * tokens * width * local, bytes_accessed=4 * tokens * width, transcendentals=0
        ),
    )(meta, *pieces, w_own, w_sib, o_own, o_sib, gain, taps, decay, tails, states, accepted)


def per_device(
    n_tensor, n_dp,
    drafted, norm_gain, w_in, conv_taps, decay, w_out, queue_tails, states, accepted, owner_map
):
    rows, steps, local = drafted.shape
    taps_n = conv_taps.shape[0]
    tail_len = queue_tails.shape[1]
    width = w_in.shape[0]
    nz = n_tensor // 2
    share = rows // n_tensor
    block = local
    me = lax.axis_index("tensor")
    z, core = me // 2, me % 2
    is_end = jnp.logical_or(z == 0, z == nz - 1)

    swap_pairs = [(t, t ^ 1) for t in range(n_tensor)]

    def permute(value, links, what):
        with jax.named_scope(what):
            return lax.ppermute(value, "tensor", links)

    def swap(value, what):
        return permute(value, swap_pairs, what)

    def chips(links):
        return [(2 * a + c, 2 * b + c) for a, b in links for c in (0, 1)]

    sizes = [share // 2, share - share // 2]
    parts = len(sizes)
    cuts = [slice(sum(sizes[:p]), sum(sizes[:p + 1])) for p in range(parts)]

    def mine(array):
        return lax.dynamic_index_in_dim(array, core, 1, keepdims=False)

    def other(array):
        return lax.dynamic_index_in_dim(array, 1 - core, 1, keepdims=False)

    by_core = drafted.reshape(nz, 2, share, steps, local)
    here, there = mine(by_core), other(by_core)
    arrived = swap(there, "swap_tokens")
    held = []
    for part in range(parts):
        cut, size = cuts[part], sizes[part]
        held.append(jnp.stack([
            here[:, cut].reshape(nz * size * steps, local),
            arrived[:, cut].reshape(nz * size * steps, local),
        ]))

    held, conv_taps, decay, queue_tails, states, owner_map = lax.optimization_barrier(
        (held, conv_taps, decay, queue_tails, states, owner_map)
    )
    small = jnp.concatenate([conv_taps.reshape(taps_n * 3, local), decay[None]], axis=0)
    small_sib = swap(small, "swap_taps")
    tails_core = jnp.transpose(queue_tails, (1, 2, 0, 3)).reshape(tail_len * 3, nz, 2, share, local)
    tails_here = lax.dynamic_index_in_dim(tails_core, core, 2, keepdims=False)
    tails_sib = swap(lax.dynamic_index_in_dim(tails_core, 1 - core, 2, keepdims=False), "swap_tails")
    states_core = states.reshape(nz, 2, share, local)
    states_sib = swap(other(states_core), "swap_states")
    states_here = mine(states_core)

    def blocked(own, sib):
        both = jnp.concatenate([own, sib], axis=-1)
        cut = both.reshape(*both.shape[:-1], 2 * local // block, block)
        return jnp.moveaxis(cut, -2, 0)

    accepted_here = mine(accepted.reshape(nz, 2, share))

    line = nz == 4
    if line:
        order = [z, z ^ 1, jnp.where(z < 2, 2, 1), jnp.where(z < 2, 3, 0)]
        ends = chips([(0, 1), (1, 0), (2, 3), (3, 2)])
        outward = chips([(1, 0), (2, 3)])
        inward = chips([(0, 1), (3, 2)])
        between = chips([(1, 2), (2, 1)])
        middle = between + [(0, 1), (1, 0), (6, 7), (7, 6)]
        across = chips([(0, 3), (3, 0)]) + [(2, 3), (3, 2), (4, 5), (5, 4)]
        skip_in = chips([(0, 2), (3, 1)])
        skip_out = chips([(2, 0), (1, 3)])
    else:
        order = [(z - k) % nz for k in range(nz)]
        ring = chips([(k, (k + 1) % nz) for k in range(nz)])
    meta = jnp.stack([is_end.astype(jnp.int32), core] + order).astype(jnp.int32)

    def ordered(array):
        return jnp.concatenate(
            [array[:, cut].reshape(-1) for cut in cuts]
        )

    def commit_order(owner_map):
        owner_core = owner_map.reshape(nz, 2, share)
        owner = jnp.concatenate([ordered(mine(owner_core)), ordered(other(owner_core))])
        sends = rows // n_dp
        target, slot = owner // rows, owner % rows
        same = target[:, None] == target[None, :]
        index = jnp.arange(rows, dtype=jnp.int32)
        rank = jnp.sum(jnp.where(same & (index[None, :] < index[:, None]), 1, 0), axis=1)
        place = target * sends + rank
        pick = place[None, :] == index[:, None]
        slot_out = jnp.sum(jnp.where(pick, slot[None, :], 0), axis=1)
        slot_in = lax.all_to_all(slot_out.reshape(n_dp, sends), "dp", split_axis=0, concat_axis=0, tiled=True)
        put = (slot_in.reshape(rows)[None, :] == index[:, None]).astype(jnp.bfloat16)
        pick = pick.astype(jnp.bfloat16)
        return pick, put

    if line:
        x0, x1 = held
        e1, m1 = permute(x0, ends, "gather0_e1"), permute(x0, middle, "gather0_m1")
        e1, m1, owner_map, w_in, w_out, small_sib, tails_sib, states_sib = lax.optimization_barrier(
            (e1, m1, owner_map, w_in, w_out, small_sib, tails_sib, states_sib)
        )
    w_own = jnp.transpose(w_in, (1, 0, 2))
    w_sib = swap(w_own, "swap_w_in")
    o_sib = swap(w_out, "swap_w_out")
    small_all = blocked(small, small_sib)
    taps_all, decay_all = small_all[:, :-1], small_all[:, -1:]
    gain = norm_gain[None]
    sides = []
    for cut, size in zip(cuts, sizes):
        sides.append((
            blocked(
                tails_here[:, :, cut].reshape(tail_len * 3, nz * size, local),
                tails_sib[:, :, cut].reshape(tail_len * 3, nz * size, local),
            ),
            blocked(
                states_here[:, cut].reshape(nz * size, local), states_sib[:, cut].reshape(nz * size, local)
            ),
            accepted_here[:, cut].reshape(nz * size, 1),
        ))

    barrier = lax.optimization_barrier

    def add(a, b):
        return (a.astype(jnp.float32) + b.astype(jnp.float32)).astype(jnp.bfloat16)

    def run(part, slots):
        tails_part, states_part, accepted_part = sides[part]
        return run_chunk(
            nz, meta, slots, w_own, w_sib, w_out, o_sib, gain, taps_all, decay_all,
            tails_part, states_part, accepted_part, steps, sizes[part], taps_n, tail_len,
        )

    if line:
        e2 = permute(m1, outward, "gather0_e2")
        m2 = permute(e1, between, "gather0_m2")
        m2, x1, sides, taps_all, decay_all, meta, owner_map = barrier(
            (m2, x1, sides, taps_all, decay_all, meta, owner_map)
        )
        pick, put = commit_order(owner_map)
        e3 = permute(m2, outward, "gather0_e3")
        g1 = permute(x1, middle, "gather1_m1")
        e2, e3, g1, x1, pick, put = barrier((e2, e3, g1, x1, pick, put))
        f1 = permute(x1, ends, "gather1_e1")
        g2, f3 = permute(x1, skip_in, "gather1_skip"), permute(x1, across, "gather1_across")
        f2 = permute(g1, outward, "gather1_e2")
        first = run(0, [(x0,), (e1,), (m1, e2), (m2, e3)])
        own0, near0, mid0, far0, commit0 = first
        mid0, far0, f1, f2, f3, g2 = barrier((mid0, far0, f1, f2, f3, g2))
        mid0_in = permute(mid0, inward, "sum0_mid_in")
        far0_in, skip0_in = permute(far0, across, "sum0_across"), permute(far0, skip_out, "sum0_skip")
        own1, near1, mid1, far1, commit1 = run(1, [(x1,), (f1,), (g1, f2), (g2, f3)])
        far1_in = permute(far1, inward, "sum1_far_in")
        near1, commit1, mid0_in, far0_in, skip0_in = barrier((near1, commit1, mid0_in, far0_in, skip0_in))
        mid0_on = permute(add(mid0, mid0_in), middle, "sum0_mid_on")
        near0, mid1, far1_in, mid0_on = barrier((near0, mid1, far1_in, mid0_on))
        mid1_in = permute(mid1, inward, "sum1_mid_in")
        near0_in = permute(near0, ends, "sum0_near")
        second = [own1, near1, mid1, far1, commit1]
        results = [first, second]
    else:
        pick, put = commit_order(owner_map)
        results = []
        for part in range(parts):
            slots = [(held[part],)]
            for _ in range(nz - 1):
                slots.append((permute(slots[-1][0], ring, f"gather{part}"),))
            results.append(run(part, slots))

    packed = jnp.concatenate([r[-1] for r in results], axis=1)
    packed = jnp.concatenate([packed[0], swap(packed[1], "swap_commit")], axis=0)
    sent = jnp.dot(pick, packed, preferred_element_type=jnp.float32).astype(jnp.bfloat16)
    if line:
        far1_on = permute(add(far1, far1_in), middle, "sum1_far_on")
        mid1, sent = barrier((add(mid1, mid1_in), sent))
    got = lax.all_to_all(sent, "dp", split_axis=0, concat_axis=0, tiled=True)
    if line:
        mid1_on = permute(mid1, middle, "sum1_mid_on")
        near1 = add(near1, jnp.where(is_end, 0, far1_on))
        near1_in = permute(near1, ends, "sum1_near")
        wide = lambda value: value.astype(jnp.float32)
        total0 = own0 + wide(near0_in) + jnp.where(is_end, wide(far0_in) + wide(skip0_in), wide(mid0_on))
        total1 = own1 + wide(near1_in) + jnp.where(is_end, 0, wide(mid1_on))
        totals = [total0, total1]
    else:
        totals = []
        for terms in results:
            flow = terms[1]
            for k in range(2, nz):
                flow = add(terms[k], permute(flow, ring, "sum"))
            totals.append(terms[0] + permute(flow, ring, "sum").astype(jnp.float32))
    mixed = jnp.concatenate(totals, axis=0).astype(jnp.bfloat16).reshape(share, steps, width)

    placed = jnp.dot(put, got, preferred_element_type=jnp.float32)
    edge = 3 * tail_len * local
    new_tails = placed[:, :edge].astype(jnp.bfloat16).reshape(rows, 3, tail_len, local)
    new_tails = jnp.transpose(new_tails, (0, 2, 1, 3))
    new_states = placed[:, edge:edge + local] + placed[:, edge + local:]
    return (mixed, new_tails, new_states)


def solution(mesh):
    return jax.shard_map(
        functools.partial(per_device, mesh.shape["tensor"], mesh.shape["dp"]),
        mesh=mesh,
        in_specs=(
            P("dp", None, "tensor"),
            P(),
            P(None, None, "tensor"),
            P(None, None, "tensor"),
            P("tensor"),
            P("tensor", None),
            P("dp", None, None, "tensor"),
            P("dp", "tensor"),
            P("dp"),
            P("dp"),
        ),
        out_specs=(
            P(("dp", "tensor"), None, None),
            P("dp", None, None, "tensor"),
            P("dp", "tensor"),
        ),
        check_vma=False,
    )
```
